768 devices in a mesh: blk: 96 (over z, y), rep: 2 (over core), slab: 4 (over x).
Axes of the slice: x: 4, y: 8, z: 12, core: 2. Of those that a mesh axis runs over, the one named last changes fastest.
Arguments:
- t2_source: bfloat16 [2304, 128, 5120], P('blk', None, ('rep', 'slab')), may hold values from -6 to 6
- integrals: bfloat16 [8, 5120, 320], P(None, ('rep', 'slab')), may hold values from -0.078125 to 0.078125
- sector_tiles: int32 [8], replicated, may hold values from 1 to 384, 1536 in all
- block_offsets: int32 [96, 2], replicated, may hold values from 0 to 1536, as said below
Outputs:
- cycle_residual: bfloat16 [1536, 128, 320], P('blk', None, ('rep', 'slab'))
The draws below stay inside these ranges and needn't reach their ends.
Inputs may be any that keep to these rules, and one draw needn't show every extreme that they name: `sector_tiles`: each of the 8 entries is at least 1, they sum to 1536, and one equals 384. block_offsets[0, 0] = 0, block_offsets[d, 1] = block_offsets[d + 1, 0], block_offsets[96 - 1, 1] = 1536; every boundary block_offsets[d, 0] lies within 4 of d * 16; some blk index holds exactly 24 blocks.
All inputs are finite; a program needn't handle non-finite values.
Results may differ from the reference program's by a relative error of at most 0.017.
Values may be sent and summed in bfloat16 or wider, within the bound.
No kernel may reach another device: no remote copies, remote signals or barrier semaphores. Data moves between devices by JAX's collectives and lax.ppermute only.
A program may use at most 32 MiB of HBM per device.

```python
import math
import jax
import jax.numpy as jnp
import numpy as np
from jax import lax

RB = 128
KC = 5120
BJ = 320
SECTORS = 8
BLK_DEV = 16
SHIFT_MOST = 4
CAP = 24
NB = 1536
SECTOR_MOST = 384
N_BLK = 96
N_REP = 2
N_SLAB = 4


def draw_block_offsets(key, part):
    key = jax.random.fold_in(key, 7)
    key_inner, key_full = jax.random.split(key)
    inner = jax.random.randint(key_inner, (N_BLK - 1,), -SHIFT_MOST, SHIFT_MOST + 1)
    zero_end = jnp.zeros((1,), jnp.int32)
    shifts = jnp.concatenate([zero_end, inner.astype(jnp.int32), zero_end])
    fullest = jax.random.randint(key_full, (), 1, N_BLK - 1)
    places = jnp.arange(N_BLK + 1, dtype=jnp.int32)
    shifts = jnp.where(places == fullest, -SHIFT_MOST, shifts)
    shifts = jnp.where(places == fullest + 1, SHIFT_MOST, shifts)
    bounds = places * BLK_DEV + shifts
    return jnp.stack([bounds[:-1], bounds[1:]], axis=1).astype(jnp.int32)


def steps_of(rng, shape, cuts, least, largest):
    gain = 1.0
    for axis_at, shards_of in cuts:
        heights = jax.random.uniform(jax.random.fold_in(jax.random.fold_in(rng, 6), axis_at), (shards_of,), jnp.float32, least / len(cuts), largest / len(cuts))
        gain = gain * jnp.repeat(jnp.exp(heights), shape[axis_at] // shards_of).reshape((-1,) + (1,) * (len(shape) - 1 - axis_at))
    return gain


def profile(count, total, most, lean):
    weights = [(1 << 20) // math.isqrt(standing ** lean) + 1 for standing in range(2, count + 1)]
    spare, holding = total - most - (count - 1), [1] * (count - 1)
    while spare > 0:
        movable = [i for i in range(count - 1) if holding[i] < most]
        pool, left = sum([weights[i] for i in movable]), spare
        for i in movable:
            extra = min(most - holding[i], max(1, left * weights[i] // pool), spare)
            holding[i] = holding[i] + extra
            spare = spare - extra
    return np.array([most] + holding)


def ragged(rng, count, total, limit, skew):
    if count == 2:
        one = jax.random.randint(rng, (), max(1, total - limit), min(limit, total - 1) + 1)
        return jnp.stack([one, total - one])
    lengths = jnp.asarray(profile(count, total, limit, skew), jnp.int32)
    pairs = (count - 1) // 2
    donor, sink = lengths[1:1 + 2 * pairs:2], lengths[2:2 + 2 * pairs:2]
    room = jnp.minimum(donor - 1, limit - sink)
    moved = jax.random.randint(jax.random.fold_in(rng, 1), (pairs,), 0, 1 << 20) % (room + 1)
    lengths = lengths.at[1:1 + 2 * pairs:2].set(donor - moved).at[2:2 + 2 * pairs:2].set(sink + moved)
    return lengths[jax.random.permutation(jax.random.fold_in(rng, 2), count)]


def normal_values(stream_key, extent, width, limit, shards=(), kind=jnp.bfloat16):
    array = jax.random.normal(stream_key, extent, jnp.float32) * width
    if len(shards) > 0:
        array = steps_of(stream_key, extent, shards, -0.22, 0.18) * array
    return jnp.clip(array, min=-limit, max=limit).astype(kind)


def setup_inputs(seed: int = 0) -> dict:
    key_list = jax.random.split(jax.random.key(seed), 5)
    t2_source = normal_values(key_list[0], (N_BLK * CAP, RB, KC), 1.0, 6.0, ((0, 96), (2, 8)))
    integrals = normal_values(key_list[1], (SECTORS, KC, BJ), KC ** -0.5, 0.078125, ((1, 8),))
    sector_tiles = ragged(key_list[2], SECTORS, NB, SECTOR_MOST, 2).astype(jnp.int32)
    block_offsets = draw_block_offsets(jax.random.fold_in(key_list[4], 71), 0)
    return {"t2_source": t2_source, "integrals": integrals, "sector_tiles": sector_tiles, "block_offsets": block_offsets}


def reference(t2_source, integrals, sector_tiles, block_offsets):
    part_count = N_REP * N_SLAB
    part_width = KC // part_count
    sector_ends = jnp.cumsum(sector_tiles).astype(jnp.int32)
    first_blocks = block_offsets[:, 0].astype(jnp.int32)

    def one_block(block):
        sector = jnp.sum((sector_ends <= block).astype(jnp.int32)).astype(jnp.int32)
        holder = (jnp.sum((first_blocks <= block).astype(jnp.int32)) - 1).astype(jnp.int32)
        first_block = lax.dynamic_index_in_dim(first_blocks, holder, 0, keepdims=False)
        source_row = (holder * CAP + block - first_block).astype(jnp.int32)
        source_tile = lax.dynamic_index_in_dim(t2_source, source_row, 0, keepdims=False)
        weights = lax.dynamic_index_in_dim(integrals, sector, 0, keepdims=False)
        source_tile = source_tile.astype(jnp.float32).reshape(RB, part_count, part_width)
        weights = weights.astype(jnp.float32).reshape(part_count, part_width, BJ)
        partial_value = jnp.einsum("rpk,pkb->prb", source_tile, weights).astype(jnp.bfloat16)
        partial_value = lax.optimization_barrier(partial_value)
        return jnp.sum(partial_value.astype(jnp.float32), axis=0).astype(jnp.bfloat16)

    return lax.map(one_block, jnp.arange(NB, dtype=jnp.int32))
```

```python
import functools

import jax
import jax.numpy as jnp
from jax import lax
from jax.experimental import pallas as pl
from jax.experimental.pallas import tpu as pltpu
from jax.sharding import PartitionSpec as P

BLK_DEV = 16
SHIFT_MOST = 4
PARTS = 8
HALF = 4


def contract_kernel(groups, tiles_ref, offsets_ref, t2_ref, weights_ref, *rest):
    outs = rest[: len(groups)]
    tiles, weights, tile_sems, weight_sems = rest[len(groups):]
    device = lax.axis_index("blk")
    rep = lax.axis_index("rep")
    first = offsets_ref[0, device]
    last = offsets_ref[1, device] - 1
    sector_count, width, _ = weights_ref.shape
    ends = []
    total = jnp.int32(0)
    for s in range(sector_count):
        total = total + tiles_ref[s]
        ends.append(total)

    blocks, sectors = [], []
    for start, count in groups:
        for j in range(count):
            block = jnp.clip(device * BLK_DEV + (start + j), first, last)
            sector = jnp.int32(0)
            for s in range(sector_count - 1):
                sector = sector + (ends[s] <= block).astype(jnp.int32)
            blocks.append(block)
            sectors.append(sector)

    def weight_copy(s):
        return pltpu.make_async_copy(weights_ref.at[s], weights.at[s], weight_sems.at[s])

    def tile_copy(j):
        return pltpu.make_async_copy(t2_ref.at[blocks[j] - first], tiles.at[j], tile_sems.at[j])

    def at_new_sector(j, step):
        if j == 0:
            step()
        else:
            pl.when(sectors[j] != sectors[j - 1])(step)

    for j in range(len(blocks)):
        at_new_sector(j, lambda: weight_copy(sectors[j]).start())
        tile_copy(j).start()

    half = width // 2
    columns = width // PARTS
    at = 0
    for g, (start, count) in enumerate(groups):
        for pair in range(count // 2):
            for j in (at, at + 1):
                at_new_sector(j, lambda: weight_copy(sectors[j]).wait())
                tile_copy(j).wait()
            for side in range(2):
                of_rep = pl.ds(pl.multiple_of((rep ^ side) * half, half), half)
                products = [
                    lax.dot_general(
                        weights[sectors[j], of_rep, :], tiles[j], (((1,), (1,)), ((), ())),
                        preferred_element_type=jnp.float32,
                    )
                    for j in (at, at + 1)
                ]
                for part in range(HALF):
                    rows = slice(part * columns, (part + 1) * columns)
                    both = jnp.concatenate([value[rows] for value in products], axis=0)
                    at_rows = slice(pair * 2 * columns, (pair + 1) * 2 * columns)
                    outs[g][side * HALF + part, at_rows, :] = both.astype(outs[g].dtype)
            at += 2


def contract(groups, sector_tiles, offsets, t2, weights):
    used = sum(count for _, count in groups)
    sectors, width, depth = weights.shape
    rows = t2.shape[1]
    shapes = [
        jax.ShapeDtypeStruct((PARTS, count * (width // PARTS), rows), jnp.bfloat16)
        for _, count in groups
    ]
    return pl.pallas_call(
        functools.partial(contract_kernel, groups),
        out_shape=shapes,
        in_specs=[
            pl.BlockSpec(memory_space=pltpu.SMEM),
            pl.BlockSpec(memory_space=pltpu.SMEM),
            pl.BlockSpec(memory_space=pltpu.HBM),
            pl.BlockSpec(memory_space=pltpu.HBM),
        ],
        out_specs=[pl.BlockSpec(memory_space=pltpu.VMEM)] * len(shapes),
        scratch_shapes=[
            pltpu.VMEM((used, rows, depth), t2.dtype),
            pltpu.VMEM((sectors, width, depth), weights.dtype),
            pltpu.SemaphoreType.DMA((used,)),
            pltpu.SemaphoreType.DMA((sectors,)),
        ],
        cost_estimate=pl.CostEstimate(
            flops=2 * used * rows * depth * width,
            bytes_accessed=2 * (used * rows * depth + used * rows * width),
            transcendentals=0,
        ),
        compiler_params=pltpu.CompilerParams(vmem_limit_bytes=52 * 1024 * 1024),
    )(sector_tiles, offsets, t2, weights)


def merge_kernel(offsets_ref, own, left, right, kept, given):
    device = lax.axis_index("blk")
    first = offsets_ref[0, device]
    end = offsets_ref[1, device]
    size, edge = own.shape[1], left.shape[1]
    columns = edge // SHIFT_MOST
    base = device * BLK_DEV
    row = lax.broadcasted_iota(jnp.int32, (edge, own.shape[2]), 0)
    below = row < (first - base) * columns
    above = row >= (end - (base + BLK_DEV - SHIFT_MOST)) * columns
    middle = slice(edge, size - edge)
    for part in range(PARTS):
        out = (kept, given)[part // HALF]
        at = part % HALF
        for mask, other, rows in (
            (below, left, slice(0, edge)),
            (above, right, slice(size - edge, size)),
        ):
            value = jnp.where(
                mask, other[part].astype(jnp.float32), own[part, rows, :].astype(jnp.float32)
            )
            out[at, rows, :] = value.astype(out.dtype)
        out[at, middle, :] = own[part, middle, :]


def merge(offsets, own, left, right):
    vmem = pl.BlockSpec(memory_space=pltpu.VMEM)
    half = jax.ShapeDtypeStruct((HALF,) + own.shape[1:], own.dtype)
    return pl.pallas_call(
        merge_kernel,
        out_shape=[half] * 2,
        in_specs=[pl.BlockSpec(memory_space=pltpu.SMEM)] + [vmem] * 3,
        out_specs=[vmem] * 2,
        cost_estimate=pl.CostEstimate(flops=0, bytes_accessed=4 * own.size, transcendentals=0),
        compiler_params=pltpu.CompilerParams(vmem_limit_bytes=8 * 1024 * 1024),
    )(offsets, own, left, right)


def shifted(block, axis, distance):
    count = lax.axis_size(axis)
    route = [(i, i + distance) for i in range(count) if 0 <= i + distance < count]
    return lax.ppermute(block, axis, route)


def per_device(t2_source, integrals, sector_tiles, block_offsets):
    offsets = jnp.swapaxes(block_offsets, 0, 1)
    weights = jnp.swapaxes(integrals, 1, 2)

    leftward, rightward = contract(
        ((-SHIFT_MOST, SHIFT_MOST), (BLK_DEV, SHIFT_MOST)), sector_tiles, offsets, t2_source, weights
    )
    from_left = shifted(rightward, "blk", 1)
    from_right = shifted(leftward, "blk", -1)
    (own,) = contract(((0, BLK_DEV),), sector_tiles, offsets, t2_source, weights)

    kept, given = merge(offsets, own, from_left, from_right)
    taken = lax.ppermute(given, "rep", [(0, 1), (1, 0)])
    chip = (kept.astype(jnp.float32) + taken.astype(jnp.float32)).astype(jnp.bfloat16)
    chunks = lax.all_to_all(chip, "slab", 0, 0, tiled=True)
    a, b, c, d = (chunks[i].astype(jnp.float32) for i in range(HALF))
    total = ((a + b) + (c + d)).astype(jnp.bfloat16)
    return jnp.swapaxes(total.reshape(BLK_DEV, -1, total.shape[1]), 1, 2)


def solution(mesh):
    in_specs = (P("blk", None, ("rep", "slab")), P(None, ("rep", "slab"), None), P(), P())
    out_specs = P("blk", None, ("rep", "slab"))
    return jax.shard_map(
        per_device, mesh=mesh, in_specs=in_specs, out_specs=out_specs, check_vma=False
    )
```

```python
import jax
import jax.numpy as jnp
from jax import lax
from jax.experimental import pallas as pl
from jax.experimental.pallas import tpu as pltpu
from jax.sharding import PartitionSpec as P

BLK_DEV = 16
SHIFT_MOST = 4
PARTS = 8
HALF = 4
MIB = 1024 * 1024


def product_pairs(weights, sectors, tiles, store):
    def dot(sector, tile):
        return lax.dot_general(
            weights[sector], tile, (((1,), (1,)), ((), ())), preferred_element_type=jnp.float32
        )

    pairs = len(tiles) // 2
    for pair in range(pairs):
        left, right = tiles[2 * pair][...], tiles[2 * pair + 1][...]
        both = dot(sectors[2 * pair], jnp.concatenate([left, right], axis=0))
        store(pair, both[:, : left.shape[0]], both[:, left.shape[0] :])

    for pair in range(pairs):
        left, right = sectors[2 * pair], sectors[2 * pair + 1]

        @pl.when(left != right)
        def _():
            store(pair, dot(left, tiles[2 * pair][...]), dot(right, tiles[2 * pair + 1][...]))


def interleaved(a, b, columns, outs, at):
    for part, out in enumerate(outs):
        rows = slice(part * columns, (part + 1) * columns)
        both = jnp.concatenate([a[rows], b[rows]], axis=0)
        out[at : at + 2 * columns, :] = both.astype(out.dtype)


def outward_kernel(
    sector_tiles, block_offsets, t2, integrals, kept, given, tiles, weights, info,
    counts, offsets, upper, count_sem, offset_sem, tile_sems, weight_sems,
):
    device = lax.axis_index("blk")
    rep = lax.axis_index("rep")
    sector_count, width, _ = integrals.shape
    reach = tiles.shape[0]
    half = width // 2
    columns = width // PARTS

    small = [
        pltpu.make_async_copy(block_offsets, offsets, offset_sem),
        pltpu.make_async_copy(sector_tiles, counts, count_sem),
    ]
    lower = pltpu.make_async_copy(
        t2.at[pl.ds(0, SHIFT_MOST)], tiles.at[pl.ds(0, SHIFT_MOST)], tile_sems.at[0]
    )
    for copy in small + [lower]:
        copy.start()
    for copy in small:
        copy.wait()

    first = offsets[0, device]
    last = offsets[1, device] - 1
    ends = []
    total = jnp.int32(0)
    for s in range(sector_count):
        total = total + counts[s]
        ends.append(total)

    def each_weight(step):
        for s in range(sector_count):
            begin = ends[s - 1] if s else jnp.int32(0)

            @pl.when((begin <= last) & (first < ends[s]))
            def _():
                for side in range(2):
                    from_row = pl.multiple_of((rep ^ side) * half, half)
                    step(
                        pltpu.make_async_copy(
                            integrals.at[s, pl.ds(from_row, half)],
                            weights.at[s, pl.ds(side * half, half)],
                            weight_sems.at[s, side],
                        )
                    )

    base = device * BLK_DEV
    each_weight(lambda copy: copy.start())
    above = pltpu.make_async_copy(
        t2.at[pl.ds(jnp.clip(base + BLK_DEV - first, 0, t2.shape[0] - SHIFT_MOST), SHIFT_MOST)],
        upper,
        tile_sems.at[1],
    )
    others = pltpu.make_async_copy(
        t2.at[pl.ds(SHIFT_MOST, reach - SHIFT_MOST)],
        tiles.at[pl.ds(SHIFT_MOST, reach - SHIFT_MOST)],
        tile_sems.at[2],
    )
    above.start()
    others.start()

    def sector_of(block):
        held = jnp.clip(block, first, last)
        sector = jnp.int32(0)
        for s in range(sector_count - 1):
            sector = sector + (ends[s] <= held).astype(jnp.int32)
        return sector

    outside = list(range(-SHIFT_MOST, 0)) + list(range(BLK_DEV, BLK_DEV + SHIFT_MOST))
    sectors = [sector_of(base + j) for j in outside]
    edges = [
        tiles.at[jnp.clip(base - SHIFT_MOST + j - first, 0, SHIFT_MOST - 1)]
        for j in range(SHIFT_MOST)
    ] + [upper.at[j] for j in range(SHIFT_MOST)]

    for j in range(BLK_DEV):
        info[j] = sector_of(base + j)
        info[BLK_DEV + j] = jnp.clip(base + j - first, 0, reach - 1)
    info[2 * BLK_DEV] = first - base
    info[2 * BLK_DEV + 1] = last + 1 - base
    info[2 * BLK_DEV + 2] = rep

    def store(pair, a, b):
        group, at = divmod(pair, SHIFT_MOST // 2)
        outs = [out.at[group, part] for out in (kept, given) for part in range(HALF)]
        interleaved(a, b, columns, outs, at * 2 * columns)

    lower.wait()
    each_weight(lambda copy: copy.wait())
    above.wait()
    product_pairs(weights, sectors, edges, store)
    others.wait()


def outward(sector_tiles, offsets, t2, integrals):
    sectors, width, depth = integrals.shape
    rows = t2.shape[1]
    out = jax.ShapeDtypeStruct((2, HALF, SHIFT_MOST * (width // PARTS), rows), jnp.bfloat16)
    hbm = pl.BlockSpec(memory_space=pltpu.HBM)
    vmem = pl.BlockSpec(memory_space=pltpu.VMEM)
    args = [
        pltpu.with_memory_space_constraint(x, pltpu.HBM)
        for x in (sector_tiles, offsets, t2, integrals)
    ]
    return pl.pallas_call(
        outward_kernel,
        out_shape=[
            out,
            out,
            jax.ShapeDtypeStruct((BLK_DEV + SHIFT_MOST, rows, depth), t2.dtype),
            jax.ShapeDtypeStruct(integrals.shape, integrals.dtype),
            pltpu.SMEM((128,), jnp.int32),
        ],
        in_specs=[hbm] * 4,
        out_specs=[vmem] * 4 + [pl.BlockSpec(memory_space=pltpu.SMEM)],
        scratch_shapes=[
            pltpu.SMEM(sector_tiles.shape, jnp.int32),
            pltpu.SMEM(offsets.shape, jnp.int32),
            pltpu.VMEM((SHIFT_MOST, rows, depth), t2.dtype),
            pltpu.SemaphoreType.DMA(()),
            pltpu.SemaphoreType.DMA(()),
            pltpu.SemaphoreType.DMA((3,)),
            pltpu.SemaphoreType.DMA((sectors, 2)),
        ],
        cost_estimate=pl.CostEstimate(
            flops=4 * SHIFT_MOST * rows * depth * width,
            bytes_accessed=2 * t2.size,
            transcendentals=0,
        ),
        compiler_params=pltpu.CompilerParams(vmem_limit_bytes=24 * MIB),
    )(*args)


def own_kernel(info, tiles, weights, partial):
    columns = weights.shape[1] // PARTS
    rep = info[2 * BLK_DEV + 2]

    def store(pair, a, b):
        outs = [partial.at[rep ^ side, part] for side in range(2) for part in range(HALF)]
        interleaved(a, b, columns, outs, pair * 2 * columns)

    sectors = [info[j] for j in range(BLK_DEV)]
    slots = [tiles.at[info[BLK_DEV + j]] for j in range(BLK_DEV)]
    product_pairs(weights, sectors, slots, store)


def own(info, tiles, weights):
    _, width, depth = weights.shape
    rows = tiles.shape[1]
    vmem = pl.BlockSpec(memory_space=pltpu.VMEM)
    return pl.pallas_call(
        own_kernel,
        out_shape=jax.ShapeDtypeStruct(
            (2, HALF, BLK_DEV * (width // PARTS), rows), jnp.bfloat16
        ),
        in_specs=[pl.BlockSpec(memory_space=pltpu.SMEM)] + [vmem] * 2,
        out_specs=vmem,
        cost_estimate=pl.CostEstimate(
            flops=2 * BLK_DEV * rows * depth * width,
            bytes_accessed=2 * (tiles.size + BLK_DEV * rows * width),
            transcendentals=0,
        ),
        compiler_params=pltpu.CompilerParams(vmem_limit_bytes=24 * MIB),
    )(pltpu.with_memory_space_constraint(info, pltpu.SMEM), tiles, weights)


def combine_kernel(info, pieces, left, right, chip):
    size, edge = chip.shape[1], left.shape[1]
    columns = edge // SHIFT_MOST
    row = lax.broadcasted_iota(jnp.int32, (edge, chip.shape[2]), 0)
    below = row < info[2 * BLK_DEV] * columns
    above = row >= (info[2 * BLK_DEV + 1] - (BLK_DEV - SHIFT_MOST)) * columns
    for part in range(HALF):
        for mask, other, rows in (
            (below, left, slice(0, edge)),
            (None, None, slice(edge, size - edge)),
            (above, right, slice(size - edge, size)),
        ):
            value = pieces[0, part, rows, :].astype(jnp.float32)
            value = value + pieces[1, part, rows, :].astype(jnp.float32)
            if mask is not None:
                value = jnp.where(mask, other[part].astype(jnp.float32), value)
            chip[part, rows, :] = value.astype(chip.dtype)


def combine(info, pieces, left, right):
    vmem = pl.BlockSpec(memory_space=pltpu.VMEM)
    return pl.pallas_call(
        combine_kernel,
        out_shape=jax.ShapeDtypeStruct(pieces.shape[1:], pieces.dtype),
        in_specs=[pl.BlockSpec(memory_space=pltpu.SMEM)] + [vmem] * 3,
        out_specs=vmem,
        cost_estimate=pl.CostEstimate(
            flops=pieces.size, bytes_accessed=4 * pieces.size, transcendentals=0
        ),
        compiler_params=pltpu.CompilerParams(vmem_limit_bytes=8 * MIB),
    )(pltpu.with_memory_space_constraint(info, pltpu.SMEM), pieces, left, right)


def shifted(block, axis, distance):
    count = lax.axis_size(axis)
    route = [(i, i + distance) for i in range(count) if 0 <= i + distance < count]
    return lax.ppermute(block, axis, route)


def swapped(block):
    return lax.ppermute(block, "rep", [(0, 1), (1, 0)])


def per_device(t2_source, integrals, sector_tiles, block_offsets):
    offsets = jnp.swapaxes(block_offsets, 0, 1)
    weights = jnp.swapaxes(integrals, 1, 2)

    kept_out, given_out, tiles, weights, info = outward(sector_tiles, offsets, t2_source, weights)
    taken_out = swapped(given_out)
    partial = own(info, tiles, weights)
    leftward, rightward = (
        (kept_out[i].astype(jnp.float32) + taken_out[i].astype(jnp.float32)).astype(jnp.bfloat16)
        for i in range(2)
    )
    leftward, rightward, partial = lax.optimization_barrier((leftward, rightward, partial))
    from_left = shifted(rightward, "blk", 1)
    from_right = shifted(leftward, "blk", -1)

    pieces = lax.all_to_all(partial, "rep", 0, 0, tiled=True)
    chip = combine(info, pieces, from_left, from_right)
    chunks = lax.all_to_all(chip, "slab", 0, 0, tiled=True)
    a, b, c, d = (chunks[i].astype(jnp.float32) for i in range(HALF))
    total = ((a + b) + (c + d)).astype(jnp.bfloat16)
    return jnp.swapaxes(total.reshape(BLK_DEV, -1, total.shape[1]), 1, 2)


def solution(mesh):
    in_specs = (P("blk", None, ("rep", "slab")), P(None, ("rep", "slab"), None), P(), P())
    out_specs = P("blk", None, ("rep", "slab"))
    return jax.shard_map(
        per_device, mesh=mesh, in_specs=in_specs, out_specs=out_specs, check_vma=False
    )
```

```python
import jax
import jax.numpy as jnp
from jax import lax
from jax.experimental import pallas as pl
from jax.experimental.pallas import tpu as pltpu
from jax.sharding import PartitionSpec as P

BLK_DEV = 16
SHIFT_MOST = 4
PARTS = 8
HALF = 4
MIB = 1024 * 1024


def product_pairs(weights, sectors, tiles, store):
    def dot(sector, tile):
        return lax.dot_general(
            weights[sector], tile, (((1,), (1,)), ((), ())), preferred_element_type=jnp.float32
        )

    pairs = len(tiles) // 2
    for pair in range(pairs):
        left, right = tiles[2 * pair][...], tiles[2 * pair + 1][...]
        both = dot(sectors[2 * pair], jnp.concatenate([left, right], axis=0))
        store(pair, both[:, : left.shape[0]], both[:, left.shape[0] :])

    for pair in range(pairs):
        left, right = sectors[2 * pair], sectors[2 * pair + 1]

        @pl.when(left != right)
        def _():
            store(pair, dot(left, tiles[2 * pair][...]), dot(right, tiles[2 * pair + 1][...]))


def interleaved(a, b, columns, outs, at):
    for part, out in enumerate(outs):
        rows = slice(part * columns, (part + 1) * columns)
        both = jnp.concatenate([a[rows], b[rows]], axis=0)
        out[at : at + 2 * columns, :] = both.astype(out.dtype)


def outward_kernel(
    sector_tiles, block_offsets, t2, integrals, kept, given, tiles, weights, info,
    counts, offsets, upper, count_sem, offset_sem, tile_sems, weight_sems,
):
    device = lax.axis_index("blk")
    rep = lax.axis_index("rep")
    sector_count, width, _ = integrals.shape
    reach = tiles.shape[0]
    half = width // 2
    columns = width // PARTS

    small = [
        pltpu.make_async_copy(block_offsets, offsets, offset_sem),
        pltpu.make_async_copy(sector_tiles, counts, count_sem),
    ]
    lower = pltpu.make_async_copy(
        t2.at[pl.ds(0, SHIFT_MOST)], tiles.at[pl.ds(0, SHIFT_MOST)], tile_sems.at[0]
    )
    for copy in small + [lower]:
        copy.start()
    for copy in small:
        copy.wait()

    first = offsets[0, device]
    last = offsets[1, device] - 1
    ends = []
    total = jnp.int32(0)
    for s in range(sector_count):
        total = total + counts[s]
        ends.append(total)

    def each_weight(step):
        for s in range(sector_count):
            begin = ends[s - 1] if s else jnp.int32(0)

            @pl.when((begin <= last) & (first < ends[s]))
            def _():
                for side in range(2):
                    from_row = pl.multiple_of((rep ^ side) * half, half)
                    step(
                        pltpu.make_async_copy(
                            integrals.at[s, pl.ds(from_row, half)],
                            weights.at[s, pl.ds(side * half, half)],
                            weight_sems.at[s, side],
                        )
                    )

    base = device * BLK_DEV
    each_weight(lambda copy: copy.start())
    above = pltpu.make_async_copy(
        t2.at[pl.ds(jnp.clip(base + BLK_DEV - first, 0, t2.shape[0] - SHIFT_MOST), SHIFT_MOST)],
        upper,
        tile_sems.at[1],
    )
    others = pltpu.make_async_copy(
        t2.at[pl.ds(SHIFT_MOST, reach - SHIFT_MOST)],
        tiles.at[pl.ds(SHIFT_MOST, reach - SHIFT_MOST)],
        tile_sems.at[2],
    )
    above.start()
    others.start()

    def sector_of(block):
        held = jnp.clip(block, first, last)
        sector = jnp.int32(0)
        for s in range(sector_count - 1):
            sector = sector + (ends[s] <= held).astype(jnp.int32)
        return sector

    outside = list(range(-SHIFT_MOST, 0)) + list(range(BLK_DEV, BLK_DEV + SHIFT_MOST))
    sectors = [sector_of(base + j) for j in outside]
    edges = [
        tiles.at[jnp.clip(base - SHIFT_MOST + j - first, 0, SHIFT_MOST - 1)]
        for j in range(SHIFT_MOST)
    ] + [upper.at[j] for j in range(SHIFT_MOST)]

    for j in range(BLK_DEV):
        info[j] = sector_of(base + j)
        info[BLK_DEV + j] = jnp.clip(base + j - first, 0, reach - 1)
    info[2 * BLK_DEV] = first - base
    info[2 * BLK_DEV + 1] = last + 1 - base
    info[2 * BLK_DEV + 2] = rep
    info[2 * BLK_DEV + 3] = device % 2

    def store(pair, a, b):
        group, at = divmod(pair, SHIFT_MOST // 2)
        turn = group ^ (device % 2)
        outs = [out.at[turn, part] for out in (kept, given) for part in range(HALF)]
        interleaved(a, b, columns, outs, at * 2 * columns)

    lower.wait()
    each_weight(lambda copy: copy.wait())
    above.wait()
    product_pairs(weights, sectors, edges, store)
    others.wait()


def outward(sector_tiles, offsets, t2, integrals):
    sectors, width, depth = integrals.shape
    rows = t2.shape[1]
    out = jax.ShapeDtypeStruct((2, HALF, SHIFT_MOST * (width // PARTS), rows), jnp.bfloat16)
    hbm = pl.BlockSpec(memory_space=pltpu.HBM)
    vmem = pl.BlockSpec(memory_space=pltpu.VMEM)
    args = [
        pltpu.with_memory_space_constraint(x, pltpu.HBM)
        for x in (sector_tiles, offsets, t2, integrals)
    ]
    return pl.pallas_call(
        outward_kernel,
        out_shape=[
            out,
            out,
            jax.ShapeDtypeStruct((BLK_DEV + SHIFT_MOST, rows, depth), t2.dtype),
            jax.ShapeDtypeStruct(integrals.shape, integrals.dtype),
            pltpu.SMEM((128,), jnp.int32),
        ],
        in_specs=[hbm] * 4,
        out_specs=[vmem] * 4 + [pl.BlockSpec(memory_space=pltpu.SMEM)],
        scratch_shapes=[
            pltpu.SMEM(sector_tiles.shape, jnp.int32),
            pltpu.SMEM(offsets.shape, jnp.int32),
            pltpu.VMEM((SHIFT_MOST, rows, depth), t2.dtype),
            pltpu.SemaphoreType.DMA(()),
            pltpu.SemaphoreType.DMA(()),
            pltpu.SemaphoreType.DMA((3,)),
            pltpu.SemaphoreType.DMA((sectors, 2)),
        ],
        cost_estimate=pl.CostEstimate(
            flops=4 * SHIFT_MOST * rows * depth * width,
            bytes_accessed=2 * t2.size,
            transcendentals=0,
        ),
        compiler_params=pltpu.CompilerParams(vmem_limit_bytes=24 * MIB),
    )(*args)


def own_kernel(info, tiles, weights, partial):
    columns = weights.shape[1] // PARTS
    rep = info[2 * BLK_DEV + 2]

    def store(pair, a, b):
        outs = [partial.at[rep ^ side, part] for side in range(2) for part in range(HALF)]
        interleaved(a, b, columns, outs, pair * 2 * columns)

    sectors = [info[j] for j in range(BLK_DEV)]
    slots = [tiles.at[info[BLK_DEV + j]] for j in range(BLK_DEV)]
    product_pairs(weights, sectors, slots, store)


def own(info, tiles, weights):
    _, width, depth = weights.shape
    rows = tiles.shape[1]
    vmem = pl.BlockSpec(memory_space=pltpu.VMEM)
    return pl.pallas_call(
        own_kernel,
        out_shape=jax.ShapeDtypeStruct(
            (2, HALF, BLK_DEV * (width // PARTS), rows), jnp.bfloat16
        ),
        in_specs=[pl.BlockSpec(memory_space=pltpu.SMEM)] + [vmem] * 2,
        out_specs=vmem,
        cost_estimate=pl.CostEstimate(
            flops=2 * BLK_DEV * rows * depth * width,
            bytes_accessed=2 * (tiles.size + BLK_DEV * rows * width),
            transcendentals=0,
        ),
        compiler_params=pltpu.CompilerParams(vmem_limit_bytes=24 * MIB),
    )(pltpu.with_memory_space_constraint(info, pltpu.SMEM), tiles, weights)


def combine_kernel(info, pieces, first, second, chip):
    size, edge = pieces.shape[2], first.shape[1]
    columns = edge // SHIFT_MOST
    row = lax.broadcasted_iota(jnp.int32, (edge, chip.shape[2]), 0)
    below = row < info[2 * BLK_DEV] * columns
    above = row >= (info[2 * BLK_DEV + 1] - (BLK_DEV - SHIFT_MOST)) * columns
    is_odd = info[2 * BLK_DEV + 3] == 1
    for part in range(HALF):
        for mask, other, rows in (
            (below, (first, second), slice(0, edge)),
            (None, None, slice(edge, size - edge)),
            (above, (second, first), slice(size - edge, size)),
        ):
            value = pieces[0, part, rows, :].astype(jnp.float32)
            value = value + pieces[1, part, rows, :].astype(jnp.float32)
            if mask is not None:
                even, odd = (x[part].astype(jnp.float32) for x in other)
                value = jnp.where(mask, jnp.where(is_odd, odd, even), value)
            chip[part, rows, :] = value.astype(chip.dtype)


def combine(info, pieces, first, second):
    vmem = pl.BlockSpec(memory_space=pltpu.VMEM)
    return pl.pallas_call(
        combine_kernel,
        out_shape=jax.ShapeDtypeStruct(pieces.shape[1:], pieces.dtype),
        in_specs=[pl.BlockSpec(memory_space=pltpu.SMEM)] + [vmem] * 3,
        out_specs=vmem,
        cost_estimate=pl.CostEstimate(
            flops=pieces.size, bytes_accessed=4 * pieces.size, transcendentals=0
        ),
        compiler_params=pltpu.CompilerParams(vmem_limit_bytes=8 * MIB),
    )(pltpu.with_memory_space_constraint(info, pltpu.SMEM), pieces, first, second)


def exchanged(block, turn):
    route = []
    for upper in range(1, lax.axis_size("blk")):
        if upper % 2 == turn:
            route += [(upper - 1, upper), (upper, upper - 1)]
    return lax.ppermute(block, "blk", route)


def swapped(block):
    return lax.ppermute(block, "rep", [(0, 1), (1, 0)])


def per_device(t2_source, integrals, sector_tiles, block_offsets):
    offsets = jnp.swapaxes(block_offsets, 0, 1)
    weights = jnp.swapaxes(integrals, 1, 2)

    kept_out, given_out, tiles, weights, info = outward(sector_tiles, offsets, t2_source, weights)
    taken_out = swapped(given_out)
    partial = own(info, tiles, weights)
    first, second = (
        (kept_out[i].astype(jnp.float32) + taken_out[i].astype(jnp.float32)).astype(jnp.bfloat16)
        for i in range(2)
    )
    first, second, partial = lax.optimization_barrier((first, second, partial))
    first = exchanged(first, 0)
    second = exchanged(second, 1)

    pieces = lax.all_to_all(partial, "rep", 0, 0, tiled=True)
    chip = combine(info, pieces, first, second)
    chunks = lax.all_to_all(chip, "slab", 0, 0, tiled=True)
    a, b, c, d = (chunks[i].astype(jnp.float32) for i in range(HALF))
    total = ((a + b) + (c + d)).astype(jnp.bfloat16)
    return jnp.swapaxes(total.reshape(BLK_DEV, -1, total.shape[1]), 1, 2)


def solution(mesh):
    in_specs = (P("blk", None, ("rep", "slab")), P(None, ("rep", "slab"), None), P(), P())
    out_specs = P("blk", None, ("rep", "slab"))
    return jax.shard_map(
        per_device, mesh=mesh, in_specs=in_specs, out_specs=out_specs, check_vma=False
    )
```

```python
import functools

import jax
import jax.numpy as jnp
from jax import lax
from jax.experimental import pallas as pl
from jax.experimental.pallas import tpu as pltpu
from jax.sharding import PartitionSpec as P

BLK_DEV = 16
SHIFT_MOST = 4
PARTS = 8
HALF = 4
MIB = 1024 * 1024
EARLY = 6


def product_pairs(weights, sectors, tiles, store):
    def dot(sector, tile):
        return lax.dot_general(
            weights[sector], tile, (((1,), (1,)), ((), ())), preferred_element_type=jnp.float32
        )

    pairs = len(tiles) // 2
    for pair in range(pairs):
        left, right = tiles[2 * pair][...], tiles[2 * pair + 1][...]
        both = dot(sectors[2 * pair], jnp.concatenate([left, right], axis=0))
        store(pair, both[:, : left.shape[0]], both[:, left.shape[0] :])

    for pair in range(pairs):
        left, right = sectors[2 * pair], sectors[2 * pair + 1]

        @pl.when(left != right)
        def _():
            store(pair, dot(left, tiles[2 * pair][...]), dot(right, tiles[2 * pair + 1][...]))


def interleaved(a, b, columns, outs, at):
    for part, out in enumerate(outs):
        rows = slice(part * columns, (part + 1) * columns)
        both = jnp.concatenate([a[rows], b[rows]], axis=0)
        out[at : at + 2 * columns, :] = both.astype(out.dtype)


def outward_kernel(
    sector_tiles, block_offsets, t2, integrals, kept, given, tiles, weights, info,
    counts, offsets, upper, count_sem, offset_sem, tile_sems, weight_sems,
):
    device = lax.axis_index("blk")
    rep = lax.axis_index("rep")
    sector_count, width, _ = integrals.shape
    reach = tiles.shape[0]
    half = width // 2
    columns = width // PARTS

    small = [
        pltpu.make_async_copy(block_offsets, offsets, offset_sem),
        pltpu.make_async_copy(sector_tiles, counts, count_sem),
    ]
    lower = pltpu.make_async_copy(
        t2.at[pl.ds(0, SHIFT_MOST)], tiles.at[pl.ds(0, SHIFT_MOST)], tile_sems.at[0]
    )
    middle = SHIFT_MOST + EARLY
    others = [
        pltpu.make_async_copy(
            t2.at[pl.ds(start, end - start)], tiles.at[pl.ds(start, end - start)], sem
        )
        for start, end, sem in (
            (SHIFT_MOST, middle, tile_sems.at[2]),
            (middle, reach, tile_sems.at[3]),
        )
    ]
    for copy in small + [lower, others[0]]:
        copy.start()
    for copy in small:
        copy.wait()

    first = offsets[0, device]
    last = offsets[1, device] - 1
    ends = []
    total = jnp.int32(0)
    for s in range(sector_count):
        total = total + counts[s]
        ends.append(total)

    def each_weight(step):
        for s in range(sector_count):
            begin = ends[s - 1] if s else jnp.int32(0)

            @pl.when((begin <= last) & (first < ends[s]))
            def _():
                for side in range(2):
                    from_row = pl.multiple_of((rep ^ side) * half, half)
                    step(
                        pltpu.make_async_copy(
                            integrals.at[s, pl.ds(from_row, half)],
                            weights.at[s, pl.ds(side * half, half)],
                            weight_sems.at[s, side],
                        )
                    )

    base = device * BLK_DEV
    each_weight(lambda copy: copy.start())
    above = pltpu.make_async_copy(
        t2.at[pl.ds(jnp.clip(base + BLK_DEV - first, 0, t2.shape[0] - SHIFT_MOST), SHIFT_MOST)],
        upper,
        tile_sems.at[1],
    )
    has_left = first < base
    has_right = last >= base + BLK_DEV
    pl.when(has_right)(above.start)
    others[1].start()

    def sector_of(block):
        held = jnp.clip(block, first, last)
        sector = jnp.int32(0)
        for s in range(sector_count - 1):
            sector = sector + (ends[s] <= held).astype(jnp.int32)
        return sector

    outside = list(range(-SHIFT_MOST, 0)) + list(range(BLK_DEV, BLK_DEV + SHIFT_MOST))
    sectors = [sector_of(base + j) for j in outside]
    edges = [
        tiles.at[jnp.clip(base - SHIFT_MOST + j - first, 0, SHIFT_MOST - 1)]
        for j in range(SHIFT_MOST)
    ] + [upper.at[j] for j in range(SHIFT_MOST)]

    for j in range(BLK_DEV):
        info[j] = sector_of(base + j)
        info[BLK_DEV + j] = jnp.clip(base + j - first, 0, reach - 1)
    info[2 * BLK_DEV] = first - base
    info[2 * BLK_DEV + 1] = last + 1 - base
    info[2 * BLK_DEV + 2] = rep
    info[2 * BLK_DEV + 3] = device % 2

    def store(group, pair, a, b):
        turn = group ^ (device % 2)
        outs = [out.at[turn, part] for out in (kept, given) for part in range(HALF)]
        interleaved(a, b, columns, outs, pair * 2 * columns)

    lower.wait()
    each_weight(lambda copy: copy.wait())


    @pl.when(has_left)
    def _():
        low = slice(0, SHIFT_MOST)
        product_pairs(weights, sectors[low], edges[low], functools.partial(store, 0))

    @pl.when(has_right)
    def _():
        above.wait()
        high = slice(SHIFT_MOST, 2 * SHIFT_MOST)
        product_pairs(weights, sectors[high], edges[high], functools.partial(store, 1))

    for copy in others:
        copy.wait()


def outward(sector_tiles, offsets, t2, integrals):
    sectors, width, depth = integrals.shape
    rows = t2.shape[1]
    out = jax.ShapeDtypeStruct((2, HALF, SHIFT_MOST * (width // PARTS), rows), jnp.bfloat16)
    hbm = pl.BlockSpec(memory_space=pltpu.HBM)
    vmem = pl.BlockSpec(memory_space=pltpu.VMEM)
    args = [
        pltpu.with_memory_space_constraint(x, pltpu.HBM)
        for x in (sector_tiles, offsets, t2, integrals)
    ]
    return pl.pallas_call(
        outward_kernel,
        out_shape=[
            out,
            out,
            jax.ShapeDtypeStruct((BLK_DEV + SHIFT_MOST, rows, depth), t2.dtype),
            jax.ShapeDtypeStruct(integrals.shape, integrals.dtype),
            pltpu.SMEM((128,), jnp.int32),
        ],
        in_specs=[hbm] * 4,
        out_specs=[vmem] * 4 + [pl.BlockSpec(memory_space=pltpu.SMEM)],
        scratch_shapes=[
            pltpu.SMEM(sector_tiles.shape, jnp.int32),
            pltpu.SMEM(offsets.shape, jnp.int32),
            pltpu.VMEM((SHIFT_MOST, rows, depth), t2.dtype),
            pltpu.SemaphoreType.DMA(()),
            pltpu.SemaphoreType.DMA(()),
            pltpu.SemaphoreType.DMA((4,)),
            pltpu.SemaphoreType.DMA((sectors, 2)),
        ],
        cost_estimate=pl.CostEstimate(
            flops=4 * SHIFT_MOST * rows * depth * width,
            bytes_accessed=2 * t2.size,
            transcendentals=0,
        ),
        compiler_params=pltpu.CompilerParams(vmem_limit_bytes=24 * MIB),
    )(*args)


def own_kernel(info, tiles, weights, partial):
    columns = weights.shape[1] // PARTS
    rep = info[2 * BLK_DEV + 2]

    def store(pair, a, b):
        outs = [partial.at[rep ^ side, part] for side in range(2) for part in range(HALF)]
        interleaved(a, b, columns, outs, pair * 2 * columns)

    sectors = [info[j] for j in range(BLK_DEV)]
    slots = [tiles.at[info[BLK_DEV + j]] for j in range(BLK_DEV)]
    product_pairs(weights, sectors, slots, store)


def own(info, tiles, weights):
    _, width, depth = weights.shape
    rows = tiles.shape[1]
    vmem = pl.BlockSpec(memory_space=pltpu.VMEM)
    return pl.pallas_call(
        own_kernel,
        out_shape=jax.ShapeDtypeStruct(
            (2, HALF, BLK_DEV * (width // PARTS), rows), jnp.bfloat16
        ),
        in_specs=[pl.BlockSpec(memory_space=pltpu.SMEM)] + [vmem] * 2,
        out_specs=vmem,
        cost_estimate=pl.CostEstimate(
            flops=2 * BLK_DEV * rows * depth * width,
            bytes_accessed=2 * (tiles.size + BLK_DEV * rows * width),
            transcendentals=0,
        ),
        compiler_params=pltpu.CompilerParams(vmem_limit_bytes=24 * MIB),
    )(pltpu.with_memory_space_constraint(info, pltpu.SMEM), tiles, weights)


def combine_kernel(info, pieces, first, second, chip):
    size, edge = pieces.shape[2], first.shape[1]
    columns = edge // SHIFT_MOST
    row = lax.broadcasted_iota(jnp.int32, (edge, chip.shape[2]), 0)
    below = row < info[2 * BLK_DEV] * columns
    above = row >= (info[2 * BLK_DEV + 1] - (BLK_DEV - SHIFT_MOST)) * columns
    is_odd = info[2 * BLK_DEV + 3] == 1
    for part in range(HALF):
        for mask, other, rows in (
            (below, (first, second), slice(0, edge)),
            (None, None, slice(edge, size - edge)),
            (above, (second, first), slice(size - edge, size)),
        ):
            value = pieces[0, part, rows, :].astype(jnp.float32)
            value = value + pieces[1, part, rows, :].astype(jnp.float32)
            if mask is not None:
                even, odd = (x[part].astype(jnp.float32) for x in other)
                value = jnp.where(mask, jnp.where(is_odd, odd, even), value)
            chip[part, rows, :] = value.astype(chip.dtype)


def combine(info, pieces, first, second):
    vmem = pl.BlockSpec(memory_space=pltpu.VMEM)
    return pl.pallas_call(
        combine_kernel,
        out_shape=jax.ShapeDtypeStruct(pieces.shape[1:], pieces.dtype),
        in_specs=[pl.BlockSpec(memory_space=pltpu.SMEM)] + [vmem] * 3,
        out_specs=vmem,
        cost_estimate=pl.CostEstimate(
            flops=pieces.size, bytes_accessed=4 * pieces.size, transcendentals=0
        ),
        compiler_params=pltpu.CompilerParams(vmem_limit_bytes=8 * MIB),
    )(pltpu.with_memory_space_constraint(info, pltpu.SMEM), pieces, first, second)


def sum_kernel(chunks, out, total, sems):
    pieces = sems.shape[0]
    size = total.shape[0] // pieces
    copies = []
    for i in range(pieces):
        rows = slice(i * size, (i + 1) * size)
        a, b, c, d = (chunks[k, rows, :].astype(jnp.float32) for k in range(HALF))
        total[rows, :] = ((a + b) + (c + d)).astype(total.dtype)
        copies.append(pltpu.make_async_copy(total.at[rows], out.at[rows], sems.at[i]))
        copies[-1].start()
    for copy in copies:
        copy.wait()


def add_up(chunks):
    _, rows, lanes = chunks.shape
    return pl.pallas_call(
        sum_kernel,
        out_shape=jax.ShapeDtypeStruct((rows, lanes), chunks.dtype),
        in_specs=[pl.BlockSpec(memory_space=pltpu.VMEM)],
        out_specs=pl.BlockSpec(memory_space=pltpu.HBM),
        scratch_shapes=[
            pltpu.VMEM((rows, lanes), chunks.dtype),
            pltpu.SemaphoreType.DMA((4,)),
        ],
        compiler_params=pltpu.CompilerParams(vmem_limit_bytes=8 * MIB),
    )(chunks)


def exchanged(block, turn):
    route = []
    for upper in range(1, lax.axis_size("blk")):
        if upper % 2 == turn:
            route += [(upper - 1, upper), (upper, upper - 1)]
    return lax.ppermute(block, "blk", route)


def swapped(block):
    return lax.ppermute(block, "rep", [(0, 1), (1, 0)])


def per_device(t2_source, integrals, sector_tiles, block_offsets):
    offsets = jnp.swapaxes(block_offsets, 0, 1)
    weights = jnp.swapaxes(integrals, 1, 2)

    kept_out, given_out, tiles, weights, info = outward(sector_tiles, offsets, t2_source, weights)
    taken_out = swapped(given_out)
    partial = own(info, tiles, weights)
    first, second = (
        (kept_out[i].astype(jnp.float32) + taken_out[i].astype(jnp.float32)).astype(jnp.bfloat16)
        for i in range(2)
    )
    first, second, partial = lax.optimization_barrier((first, second, partial))
    first = exchanged(first, 0)
    second = exchanged(second, 1)

    pieces = lax.all_to_all(partial, "rep", 0, 0, tiled=True)
    chip = combine(info, pieces, first, second)
    chunks = lax.all_to_all(chip, "slab", 0, 0, tiled=True)
    total = add_up(chunks)
    return jnp.swapaxes(total.reshape(BLK_DEV, -1, total.shape[1]), 1, 2)


def solution(mesh):
    in_specs = (P("blk", None, ("rep", "slab")), P(None, ("rep", "slab"), None), P(), P())
    out_specs = P("blk", None, ("rep", "slab"))
    return jax.shard_map(
        per_device, mesh=mesh, in_specs=in_specs, out_specs=out_specs, check_vma=False
    )
```

```python
import functools

import jax
import jax.numpy as jnp
from jax import lax
from jax.experimental import pallas as pl
from jax.experimental.pallas import tpu as pltpu
from jax.sharding import PartitionSpec as P

BLK_DEV = 16
SHIFT_MOST = 4
PARTS = 8
HALF = 4
MIB = 1024 * 1024
EARLY = 6


def product_pairs(weights, sectors, tiles, store):
    def dot(sector, tile):
        return lax.dot_general(
            weights[sector], tile, (((1,), (1,)), ((), ())), preferred_element_type=jnp.float32
        )

    pairs = len(tiles) // 2
    for pair in range(pairs):
        left, right = tiles[2 * pair][...], tiles[2 * pair + 1][...]
        both = dot(sectors[2 * pair], jnp.concatenate([left, right], axis=0))
        store(pair, both[:, : left.shape[0]], both[:, left.shape[0] :])

    for pair in range(pairs):
        left, right = sectors[2 * pair], sectors[2 * pair + 1]

        @pl.when(left != right)
        def _():
            store(pair, dot(left, tiles[2 * pair][...]), dot(right, tiles[2 * pair + 1][...]))


def interleaved(a, b, columns, outs, at):
    for part, out in enumerate(outs):
        rows = slice(part * columns, (part + 1) * columns)
        both = jnp.concatenate([a[rows], b[rows]], axis=0)
        out[at : at + 2 * columns, :] = both.astype(out.dtype)


def outward_kernel(
    sector_tiles, block_offsets, t2, integrals, kept, given, tiles, weights, info,
    counts, offsets, upper, count_sem, offset_sem, tile_sems, weight_sems,
):
    device = lax.axis_index("blk")
    rep = lax.axis_index("rep")
    sector_count, width, _ = integrals.shape
    reach = tiles.shape[0]
    half = width // 2
    columns = width // PARTS

    small = [
        pltpu.make_async_copy(block_offsets, offsets, offset_sem),
        pltpu.make_async_copy(sector_tiles, counts, count_sem),
    ]
    lower = pltpu.make_async_copy(
        t2.at[pl.ds(0, SHIFT_MOST)], tiles.at[pl.ds(0, SHIFT_MOST)], tile_sems.at[0]
    )
    middle = SHIFT_MOST + EARLY
    others = [
        pltpu.make_async_copy(
            t2.at[pl.ds(start, end - start)], tiles.at[pl.ds(start, end - start)], sem
        )
        for start, end, sem in (
            (SHIFT_MOST, middle, tile_sems.at[2]),
            (middle, reach, tile_sems.at[3]),
        )
    ]
    for copy in small + [lower, others[0]]:
        copy.start()
    for copy in small:
        copy.wait()

    first = offsets[0, device]
    last = offsets[1, device] - 1
    ends = []
    total = jnp.int32(0)
    for s in range(sector_count):
        total = total + counts[s]
        ends.append(total)

    def each_weight(step):
        for s in range(sector_count):
            begin = ends[s - 1] if s else jnp.int32(0)

            @pl.when((begin <= last) & (first < ends[s]))
            def _():
                for side in range(2):
                    from_row = pl.multiple_of((rep ^ side) * half, half)
                    step(
                        pltpu.make_async_copy(
                            integrals.at[s, pl.ds(from_row, half)],
                            weights.at[s, pl.ds(side * half, half)],
                            weight_sems.at[s, side],
                        )
                    )

    base = device * BLK_DEV
    each_weight(lambda copy: copy.start())
    above = pltpu.make_async_copy(
        t2.at[pl.ds(jnp.clip(base + BLK_DEV - first, 0, t2.shape[0] - SHIFT_MOST), SHIFT_MOST)],
        upper,
        tile_sems.at[1],
    )
    has_left = first < base
    has_right = last >= base + BLK_DEV
    pl.when(has_right)(above.start)
    others[1].start()

    def sector_of(block):
        held = jnp.clip(block, first, last)
        sector = jnp.int32(0)
        for s in range(sector_count - 1):
            sector = sector + (ends[s] <= held).astype(jnp.int32)
        return sector

    outside = list(range(-SHIFT_MOST, 0)) + list(range(BLK_DEV, BLK_DEV + SHIFT_MOST))
    sectors = [sector_of(base + j) for j in outside]
    edges = [
        tiles.at[jnp.clip(base - SHIFT_MOST + j - first, 0, SHIFT_MOST - 1)]
        for j in range(SHIFT_MOST)
    ] + [upper.at[j] for j in range(SHIFT_MOST)]

    for j in range(BLK_DEV):
        info[j] = sector_of(base + j)
        info[BLK_DEV + j] = jnp.clip(base + j - first, 0, reach - 1)
    info[2 * BLK_DEV] = first - base
    info[2 * BLK_DEV + 1] = last + 1 - base
    info[2 * BLK_DEV + 2] = rep
    info[2 * BLK_DEV + 3] = device % 2

    def store(group, pair, a, b):
        turn = group ^ (device % 2)
        outs = [out.at[turn, part] for out in (kept, given) for part in range(HALF)]
        interleaved(a, b, columns, outs, pair * 2 * columns)

    lower.wait()
    each_weight(lambda copy: copy.wait())


    @pl.when(has_left)
    def _():
        low = slice(0, SHIFT_MOST)
        product_pairs(weights, sectors[low], edges[low], functools.partial(store, 0))

    @pl.when(has_right)
    def _():
        above.wait()
        high = slice(SHIFT_MOST, 2 * SHIFT_MOST)
        product_pairs(weights, sectors[high], edges[high], functools.partial(store, 1))

    for copy in others:
        copy.wait()


def outward(sector_tiles, offsets, t2, integrals):
    sectors, width, depth = integrals.shape
    rows = t2.shape[1]
    out = jax.ShapeDtypeStruct((2, HALF, SHIFT_MOST * (width // PARTS), rows), jnp.bfloat16)
    hbm = pl.BlockSpec(memory_space=pltpu.HBM)
    vmem = pl.BlockSpec(memory_space=pltpu.VMEM)
    args = [
        pltpu.with_memory_space_constraint(x, pltpu.HBM)
        for x in (sector_tiles, offsets, t2, integrals)
    ]
    return pl.pallas_call(
        outward_kernel,
        out_shape=[
            out,
            out,
            jax.ShapeDtypeStruct((BLK_DEV + SHIFT_MOST, rows, depth), t2.dtype),
            jax.ShapeDtypeStruct(integrals.shape, integrals.dtype),
            pltpu.SMEM((128,), jnp.int32),
        ],
        in_specs=[hbm] * 4,
        out_specs=[vmem] * 4 + [pl.BlockSpec(memory_space=pltpu.SMEM)],
        scratch_shapes=[
            pltpu.SMEM(sector_tiles.shape, jnp.int32),
            pltpu.SMEM(offsets.shape, jnp.int32),
            pltpu.VMEM((SHIFT_MOST, rows, depth), t2.dtype),
            pltpu.SemaphoreType.DMA(()),
            pltpu.SemaphoreType.DMA(()),
            pltpu.SemaphoreType.DMA((4,)),
            pltpu.SemaphoreType.DMA((sectors, 2)),
        ],
        cost_estimate=pl.CostEstimate(
            flops=4 * SHIFT_MOST * rows * depth * width,
            bytes_accessed=2 * t2.size,
            transcendentals=0,
        ),
        compiler_params=pltpu.CompilerParams(vmem_limit_bytes=24 * MIB),
    )(*args)


def own_kernel(info, tiles, weights, partial):
    columns = weights.shape[1] // PARTS
    rep = info[2 * BLK_DEV + 2]

    def store(pair, a, b):
        outs = [partial.at[rep ^ side, part] for side in range(2) for part in range(HALF)]
        interleaved(a, b, columns, outs, pair * 2 * columns)

    sectors = [info[j] for j in range(BLK_DEV)]
    slots = [tiles.at[info[BLK_DEV + j]] for j in range(BLK_DEV)]
    product_pairs(weights, sectors, slots, store)


def own(info, tiles, weights):
    _, width, depth = weights.shape
    rows = tiles.shape[1]
    vmem = pl.BlockSpec(memory_space=pltpu.VMEM)
    return pl.pallas_call(
        own_kernel,
        out_shape=jax.ShapeDtypeStruct(
            (2, HALF, BLK_DEV * (width // PARTS), rows), jnp.bfloat16
        ),
        in_specs=[pl.BlockSpec(memory_space=pltpu.SMEM)] + [vmem] * 2,
        out_specs=vmem,
        cost_estimate=pl.CostEstimate(
            flops=2 * BLK_DEV * rows * depth * width,
            bytes_accessed=2 * (tiles.size + BLK_DEV * rows * width),
            transcendentals=0,
        ),
        compiler_params=pltpu.CompilerParams(vmem_limit_bytes=24 * MIB),
    )(pltpu.with_memory_space_constraint(info, pltpu.SMEM), tiles, weights)


def combine_kernel(info, first, second, pieces, chip):
    size, edge = pieces.shape[2], first.shape[1]
    columns = edge // SHIFT_MOST
    row = lax.broadcasted_iota(jnp.int32, (edge, pieces.shape[3]), 0)
    below = row < info[2 * BLK_DEV] * columns
    above = row >= (info[2 * BLK_DEV + 1] - (BLK_DEV - SHIFT_MOST)) * columns

    def own(part, rows):
        value = pieces[0, part, rows, :].astype(jnp.float32)
        return value + pieces[1, part, rows, :].astype(jnp.float32)

    for part in range(HALF):
        rows = slice(edge, size - edge)
        chip[part, rows, :] = own(part, rows).astype(chip.dtype)

    for odd, (left, right) in enumerate(((first, second), (second, first))):

        @pl.when(info[2 * BLK_DEV + 3] == odd)
        def _():
            for part in range(HALF):
                for mask, other, rows in (
                    (below, left, slice(0, edge)),
                    (above, right, slice(size - edge, size)),
                ):
                    value = jnp.where(mask, other[part].astype(jnp.float32), own(part, rows))
                    chip[part, rows, :] = value.astype(chip.dtype)


def combine(info, pieces, first, second):
    vmem = pl.BlockSpec(memory_space=pltpu.VMEM)
    return pl.pallas_call(
        combine_kernel,
        out_shape=jax.ShapeDtypeStruct(pieces.shape[1:], pieces.dtype),
        in_specs=[pl.BlockSpec(memory_space=pltpu.SMEM)] + [vmem] * 3,
        out_specs=vmem,
        cost_estimate=pl.CostEstimate(
            flops=pieces.size, bytes_accessed=4 * pieces.size, transcendentals=0
        ),
        compiler_params=pltpu.CompilerParams(vmem_limit_bytes=8 * MIB),
    )(pltpu.with_memory_space_constraint(info, pltpu.SMEM), first, second, pieces)


def sum_kernel(chunks, out, total, sems):
    pieces = sems.shape[0]
    size = total.shape[0] // pieces
    copies = []
    for i in range(pieces):
        rows = slice(i * size, (i + 1) * size)
        a, b, c, d = (chunks[k, rows, :].astype(jnp.float32) for k in range(HALF))
        total[rows, :] = ((a + b) + (c + d)).astype(total.dtype)
        copies.append(pltpu.make_async_copy(total.at[rows], out.at[rows], sems.at[i]))
        copies[-1].start()
    for copy in copies:
        copy.wait()


def add_up(chunks):
    _, rows, lanes = chunks.shape
    return pl.pallas_call(
        sum_kernel,
        out_shape=jax.ShapeDtypeStruct((rows, lanes), chunks.dtype),
        in_specs=[pl.BlockSpec(memory_space=pltpu.VMEM)],
        out_specs=pl.BlockSpec(memory_space=pltpu.HBM),
        scratch_shapes=[
            pltpu.VMEM((rows, lanes), chunks.dtype),
            pltpu.SemaphoreType.DMA((4,)),
        ],
        compiler_params=pltpu.CompilerParams(vmem_limit_bytes=8 * MIB),
    )(chunks)


def exchanged(block, turn):
    route = []
    for upper in range(1, lax.axis_size("blk")):
        if upper % 2 == turn:
            route += [(upper - 1, upper), (upper, upper - 1)]
    return lax.ppermute(block, "blk", route)


def swapped(block):
    return lax.ppermute(block, "rep", [(0, 1), (1, 0)])


def per_device(t2_source, integrals, sector_tiles, block_offsets):
    offsets = jnp.swapaxes(block_offsets, 0, 1)
    weights = jnp.swapaxes(integrals, 1, 2)

    kept_out, given_out, tiles, weights, info = outward(sector_tiles, offsets, t2_source, weights)
    taken_out = swapped(given_out)
    partial = own(info, tiles, weights)
    first, second = (
        (kept_out[i].astype(jnp.float32) + taken_out[i].astype(jnp.float32)).astype(jnp.bfloat16)
        for i in range(2)
    )
    first, second, partial = lax.optimization_barrier((first, second, partial))
    first = exchanged(first, 0)
    second = exchanged(second, 1)

    pieces = lax.all_to_all(partial, "rep", 0, 0, tiled=True)
    chip = combine(info, pieces, first, second)
    chunks = lax.all_to_all(chip, "slab", 0, 0, tiled=True)
    total = add_up(chunks)
    return jnp.swapaxes(total.reshape(BLK_DEV, -1, total.shape[1]), 1, 2)


def solution(mesh):
    in_specs = (P("blk", None, ("rep", "slab")), P(None, ("rep", "slab"), None), P(), P())
    out_specs = P("blk", None, ("rep", "slab"))
    return jax.shard_map(
        per_device, mesh=mesh, in_specs=in_specs, out_specs=out_specs, check_vma=False
    )
```

```python
import functools

import jax
import jax.numpy as jnp
from jax import lax
from jax.experimental import pallas as pl
from jax.experimental.pallas import tpu as pltpu
from jax.sharding import PartitionSpec as P

BLK_DEV = 16
SHIFT_MOST = 4
PARTS = 8
HALF = 4
MIB = 1024 * 1024
EARLY = 6


def product_pairs(weights, sectors, tiles, store):
    def dot(sector, tile):
        return lax.dot_general(
            weights[sector], tile, (((1,), (1,)), ((), ())), preferred_element_type=jnp.float32
        )

    pairs = len(tiles) // 2
    for pair in range(pairs):
        left, right = tiles[2 * pair][...], tiles[2 * pair + 1][...]
        both = dot(sectors[2 * pair], jnp.concatenate([left, right], axis=0))
        store(pair, both[:, : left.shape[0]], both[:, left.shape[0] :])

    for pair in range(pairs):
        left, right = sectors[2 * pair], sectors[2 * pair + 1]

        @pl.when(left != right)
        def _():
            store(pair, dot(left, tiles[2 * pair][...]), dot(right, tiles[2 * pair + 1][...]))


def interleaved(a, b, columns, outs, at):
    for part, out in enumerate(outs):
        rows = slice(part * columns, (part + 1) * columns)
        both = jnp.concatenate([a[rows], b[rows]], axis=0)
        out[at : at + 2 * columns, :] = both.astype(out.dtype)


def outward_kernel(
    sector_tiles, block_offsets, t2, integrals, kept, given, tiles, weights, info,
    counts, offsets, upper, count_sem, offset_sem, tile_sems, weight_sems,
):
    device = lax.axis_index("blk")
    rep = lax.axis_index("rep")
    sector_count, width, _ = integrals.shape
    reach = tiles.shape[0]
    half = width // 2
    columns = width // PARTS

    small = [
        pltpu.make_async_copy(block_offsets, offsets, offset_sem),
        pltpu.make_async_copy(sector_tiles, counts, count_sem),
    ]
    lower = pltpu.make_async_copy(
        t2.at[pl.ds(0, SHIFT_MOST)], tiles.at[pl.ds(0, SHIFT_MOST)], tile_sems.at[0]
    )
    middle = SHIFT_MOST + EARLY
    others = [
        pltpu.make_async_copy(
            t2.at[pl.ds(start, end - start)], tiles.at[pl.ds(start, end - start)], sem
        )
        for start, end, sem in (
            (SHIFT_MOST, middle, tile_sems.at[2]),
            (middle, reach, tile_sems.at[3]),
        )
    ]
    for copy in small + [lower, others[0]]:
        copy.start()
    for copy in small:
        copy.wait()

    first = offsets[0, device]
    last = offsets[1, device] - 1
    ends = []
    total = jnp.int32(0)
    for s in range(sector_count):
        total = total + counts[s]
        ends.append(total)

    def each_weight(step):
        for s in range(sector_count):
            begin = ends[s - 1] if s else jnp.int32(0)

            @pl.when((begin <= last) & (first < ends[s]))
            def _():
                for side in range(2):
                    from_row = pl.multiple_of((rep ^ side) * half, half)
                    step(
                        pltpu.make_async_copy(
                            integrals.at[s, pl.ds(from_row, half)],
                            weights.at[s, pl.ds(side * half, half)],
                            weight_sems.at[s, side],
                        )
                    )

    base = device * BLK_DEV
    each_weight(lambda copy: copy.start())
    above = pltpu.make_async_copy(
        t2.at[pl.ds(jnp.clip(base + BLK_DEV - first, 0, t2.shape[0] - SHIFT_MOST), SHIFT_MOST)],
        upper,
        tile_sems.at[1],
    )
    has_left = first < base
    has_right = last >= base + BLK_DEV
    pl.when(has_right)(above.start)
    others[1].start()

    def sector_of(block):
        held = jnp.clip(block, first, last)
        sector = jnp.int32(0)
        for s in range(sector_count - 1):
            sector = sector + (ends[s] <= held).astype(jnp.int32)
        return sector

    outside = list(range(-SHIFT_MOST, 0)) + list(range(BLK_DEV, BLK_DEV + SHIFT_MOST))
    sectors = [sector_of(base + j) for j in outside]
    edges = [
        tiles.at[jnp.clip(base - SHIFT_MOST + j - first, 0, SHIFT_MOST - 1)]
        for j in range(SHIFT_MOST)
    ] + [upper.at[j] for j in range(SHIFT_MOST)]

    for j in range(BLK_DEV):
        info[j] = sector_of(base + j)
        info[BLK_DEV + j] = jnp.clip(base + j - first, 0, reach - 1)
    info[2 * BLK_DEV] = first - base
    info[2 * BLK_DEV + 1] = last + 1 - base
    info[2 * BLK_DEV + 2] = rep
    info[2 * BLK_DEV + 3] = device % 2

    def store(group, pair, a, b):
        turn = group ^ (device % 2)
        outs = [out.at[turn, part] for out in (kept, given) for part in range(HALF)]
        interleaved(a, b, columns, outs, pair * 2 * columns)

    lower.wait()
    each_weight(lambda copy: copy.wait())


    @pl.when(has_left)
    def _():
        low = slice(0, SHIFT_MOST)
        product_pairs(weights, sectors[low], edges[low], functools.partial(store, 0))

    @pl.when(has_right)
    def _():
        above.wait()
        high = slice(SHIFT_MOST, 2 * SHIFT_MOST)
        product_pairs(weights, sectors[high], edges[high], functools.partial(store, 1))

    for copy in others:
        copy.wait()


def outward(sector_tiles, offsets, t2, integrals):
    sectors, width, depth = integrals.shape
    rows = t2.shape[1]
    out = jax.ShapeDtypeStruct((2, HALF, SHIFT_MOST * (width // PARTS), rows), jnp.bfloat16)
    hbm = pl.BlockSpec(memory_space=pltpu.HBM)
    vmem = pl.BlockSpec(memory_space=pltpu.VMEM)
    args = [
        pltpu.with_memory_space_constraint(x, pltpu.HBM)
        for x in (sector_tiles, offsets, t2, integrals)
    ]
    return pl.pallas_call(
        outward_kernel,
        out_shape=[
            out,
            out,
            jax.ShapeDtypeStruct((BLK_DEV + SHIFT_MOST, rows, depth), t2.dtype),
            jax.ShapeDtypeStruct(integrals.shape, integrals.dtype),
            pltpu.SMEM((128,), jnp.int32),
        ],
        in_specs=[hbm] * 4,
        out_specs=[vmem] * 4 + [pl.BlockSpec(memory_space=pltpu.SMEM)],
        scratch_shapes=[
            pltpu.SMEM(sector_tiles.shape, jnp.int32),
            pltpu.SMEM(offsets.shape, jnp.int32),
            pltpu.VMEM((SHIFT_MOST, rows, depth), t2.dtype),
            pltpu.SemaphoreType.DMA(()),
            pltpu.SemaphoreType.DMA(()),
            pltpu.SemaphoreType.DMA((4,)),
            pltpu.SemaphoreType.DMA((sectors, 2)),
        ],
        cost_estimate=pl.CostEstimate(
            flops=4 * SHIFT_MOST * rows * depth * width,
            bytes_accessed=2 * t2.size,
            transcendentals=0,
        ),
        compiler_params=pltpu.CompilerParams(vmem_limit_bytes=24 * MIB),
    )(*args)


def own_kernel(info, tiles, weights, partial):
    columns = weights.shape[1] // PARTS
    rep = info[2 * BLK_DEV + 2]

    def store(pair, a, b):
        outs = [partial.at[rep ^ side, part] for side in range(2) for part in range(HALF)]
        interleaved(a, b, columns, outs, pair * 2 * columns)

    sectors = [info[j] for j in range(BLK_DEV)]
    slots = [tiles.at[info[BLK_DEV + j]] for j in range(BLK_DEV)]
    product_pairs(weights, sectors, slots, store)


def own(info, tiles, weights):
    _, width, depth = weights.shape
    rows = tiles.shape[1]
    vmem = pl.BlockSpec(memory_space=pltpu.VMEM)
    return pl.pallas_call(
        own_kernel,
        out_shape=jax.ShapeDtypeStruct(
            (2, HALF, BLK_DEV * (width // PARTS), rows), jnp.bfloat16
        ),
        in_specs=[pl.BlockSpec(memory_space=pltpu.SMEM)] + [vmem] * 2,
        out_specs=vmem,
        cost_estimate=pl.CostEstimate(
            flops=2 * BLK_DEV * rows * depth * width,
            bytes_accessed=2 * (tiles.size + BLK_DEV * rows * width),
            transcendentals=0,
        ),
        compiler_params=pltpu.CompilerParams(vmem_limit_bytes=24 * MIB),
    )(pltpu.with_memory_space_constraint(info, pltpu.SMEM), tiles, weights)


def combine_kernel(info, first, second, pieces, chip):
    size, edge = pieces.shape[2], first.shape[1]
    columns = edge // SHIFT_MOST
    row = lax.broadcasted_iota(jnp.int32, (edge, pieces.shape[3]), 0)
    below = row < info[2 * BLK_DEV] * columns
    above = row >= (info[2 * BLK_DEV + 1] - (BLK_DEV - SHIFT_MOST)) * columns

    def own(part, rows):
        value = pieces[0, part, rows, :].astype(jnp.float32)
        return value + pieces[1, part, rows, :].astype(jnp.float32)

    for part in range(HALF):
        rows = slice(edge, size - edge)
        chip[part, rows, :] = own(part, rows).astype(chip.dtype)

    for odd, (left, right) in enumerate(((first, second), (second, first))):

        @pl.when(info[2 * BLK_DEV + 3] == odd)
        def _():
            for part in range(HALF):
                for mask, other, rows in (
                    (below, left, slice(0, edge)),
                    (above, right, slice(size - edge, size)),
                ):
                    value = jnp.where(mask, other[part].astype(jnp.float32), own(part, rows))
                    chip[part, rows, :] = value.astype(chip.dtype)


def combine(info, pieces, first, second):
    vmem = pl.BlockSpec(memory_space=pltpu.VMEM)
    return pl.pallas_call(
        combine_kernel,
        out_shape=jax.ShapeDtypeStruct(pieces.shape[1:], pieces.dtype),
        in_specs=[pl.BlockSpec(memory_space=pltpu.SMEM)] + [vmem] * 3,
        out_specs=vmem,
        cost_estimate=pl.CostEstimate(
            flops=pieces.size, bytes_accessed=4 * pieces.size, transcendentals=0
        ),
        compiler_params=pltpu.CompilerParams(vmem_limit_bytes=8 * MIB),
    )(pltpu.with_memory_space_constraint(info, pltpu.SMEM), first, second, pieces)


def sum_kernel(chunks, out, total, sems):
    pieces = sems.shape[0]
    size = total.shape[0] // pieces
    copies = []
    for i in range(pieces):
        rows = slice(i * size, (i + 1) * size)
        a, b, c, d = (chunks[k, rows, :].astype(jnp.float32) for k in range(HALF))
        total[rows, :] = ((a + b) + (c + d)).astype(total.dtype)
        copies.append(pltpu.make_async_copy(total.at[rows], out.at[rows], sems.at[i]))
        copies[-1].start()
    for copy in copies:
        copy.wait()


def add_up(chunks):
    _, rows, lanes = chunks.shape
    return pl.pallas_call(
        sum_kernel,
        out_shape=jax.ShapeDtypeStruct((rows, lanes), chunks.dtype),
        in_specs=[pl.BlockSpec(memory_space=pltpu.VMEM)],
        out_specs=pl.BlockSpec(memory_space=pltpu.HBM),
        scratch_shapes=[
            pltpu.VMEM((rows, lanes), chunks.dtype),
            pltpu.SemaphoreType.DMA((2,)),
        ],
        compiler_params=pltpu.CompilerParams(vmem_limit_bytes=8 * MIB),
    )(chunks)


def exchanged(block, turn):
    route = []
    for upper in range(1, lax.axis_size("blk")):
        if upper % 2 == turn:
            route += [(upper - 1, upper), (upper, upper - 1)]
    return lax.ppermute(block, "blk", route)


def swapped(block):
    return lax.ppermute(block, "rep", [(0, 1), (1, 0)])


def per_device(t2_source, integrals, sector_tiles, block_offsets):
    offsets = jnp.swapaxes(block_offsets, 0, 1)
    weights = jnp.swapaxes(integrals, 1, 2)

    kept_out, given_out, tiles, weights, info = outward(sector_tiles, offsets, t2_source, weights)
    taken_out = swapped(given_out)
    partial = own(info, tiles, weights)
    first, second = (
        (kept_out[i].astype(jnp.float32) + taken_out[i].astype(jnp.float32)).astype(jnp.bfloat16)
        for i in range(2)
    )
    first, second, partial = lax.optimization_barrier((first, second, partial))
    first = exchanged(first, 0)
    second = exchanged(second, 1)

    pieces = lax.all_to_all(partial, "rep", 0, 0, tiled=True)
    chip = combine(info, pieces, first, second)
    chunks = lax.all_to_all(chip, "slab", 0, 0, tiled=True)
    total = add_up(chunks)
    return jnp.swapaxes(total.reshape(BLK_DEV, -1, total.shape[1]), 1, 2)


def solution(mesh):
    in_specs = (P("blk", None, ("rep", "slab")), P(None, ("rep", "slab"), None), P(), P())
    out_specs = P("blk", None, ("rep", "slab"))
    return jax.shard_map(
        per_device, mesh=mesh, in_specs=in_specs, out_specs=out_specs, check_vma=False
    )
```
